32 devices in a mesh: dp: 16 (over z, y, core), mp: 2 (over x).
Axes of the slice: x: 2, y: 2, z: 4, core: 2. Of those that a mesh axis runs over, the one named last changes fastest.
Arguments:
- activations: bfloat16 [2, 32, 384, 14336], P(None, 'dp', None, 'mp'), may hold values from -6 to 6
- out_grads: bfloat16 [2, 32, 384, 4096], P(None, 'dp', None, 'mp'), may hold values from -6 to 6
- proj_in: bfloat16 [14336, 64], P('mp'), may hold values from -0.046875 to 0.046875
- proj_out: bfloat16 [4096, 64], P('mp'), may hold values from -0.09375 to 0.09375
- store: bfloat16 [2, 8192, 4096], P(None, ('dp', 'mp')), may hold values from -0.09375 to 0.09375
- ckpt_rate: float32 [2], replicated, may hold values from 0.5 to 2
- store_group: int32 [8192], P(('dp', 'mp')), may hold values from 0 to 15
Outputs:
- scores: float32 [32, 8192], P(None, ('dp', 'mp'))
- group_scores: float32 [32, 16], replicated
The draws below stay inside these ranges and needn't reach their ends.
All inputs are finite; a program needn't handle non-finite values.
Results may differ from the reference program's by a relative error of at most 0.005.
Values may be sent and summed in bfloat16 or wider, within the bound.
A program may use at most 64 MiB of HBM per device.

```python
import math
import jax
import jax.numpy as jnp
from jax import lax

D = 4096
FF = 14336
RANK = 64
SEQ = 384
GROUPS = 16
EXAMPLES = 32
STORE = 8192


def plant(values, rng, least, largest):
    shape = values.shape
    spot = [jax.random.randint(jax.random.fold_in(rng, axis), (), 0, shape[axis]) for axis in range(len(shape))]
    values = values.at[tuple(spot)].set(least)
    longest = shape.index(max(shape))
    spot[longest] = (spot[longest] + 1) % shape[longest]
    return values.at[tuple(spot)].set(largest)


def block_levels(own_key, extent, cuts, low, high):
    def one(axis_at, parts):
        steps = jax.random.uniform(jax.random.fold_in(jax.random.fold_in(own_key, 6), axis_at), (parts,), jnp.float32, low / len(cuts), high / len(cuts))
        return jnp.repeat(jnp.exp(steps), extent[axis_at] // parts).reshape((-1,) + (1,) * (len(extent) - axis_at - 1))

    factor_of = one(*cuts[0])
    for cut in cuts[1:]:
        factor_of = factor_of * one(*cut)
    return factor_of


def bell_draw(key, shape, scale, bound, cuts=(), kind=jnp.bfloat16):
    entries = scale * jax.random.normal(key, shape, jnp.float32)
    if cuts:
        entries = entries * block_levels(key, shape, cuts, -0.22, 0.18)
    return jnp.clip(entries, -bound, bound).astype(kind)


def setup_inputs(seed: int = 0) -> dict:
    arg_keys = jax.random.split(jax.random.key(seed), 8)
    return {
        "activations": bell_draw(arg_keys[0], (2, EXAMPLES, SEQ, FF), 1.0, 6.0, ((1, 16), (3, 2))),
        "out_grads": bell_draw(arg_keys[1], (2, EXAMPLES, SEQ, D), 1.0, 6.0, ((1, 16), (3, 2))),
        "proj_in": bell_draw(arg_keys[2], (FF, RANK), FF ** -0.5, 0.046875, ((0, 2),)),
        "proj_out": bell_draw(arg_keys[3], (D, RANK), D ** -0.5, 0.09375, ((0, 2),)),
        "store": bell_draw(arg_keys[4], (2, STORE, RANK * RANK), (RANK * RANK) ** -0.5, 0.09375, ((1, 32),)),
        "ckpt_rate": jnp.clip(jnp.exp(jax.random.uniform(arg_keys[5], (2,), jnp.float32, math.log(0.5), math.log(2.0))), 0.5, 2.0),
        "store_group": plant(jax.random.randint(arg_keys[6], (STORE,), 0, GROUPS), jax.random.fold_in(arg_keys[6], 1), 0, GROUPS - 1).astype(jnp.int32),
    }


def reference(activations, out_grads, proj_in, proj_out, store, ckpt_rate, store_group):
    queries = []
    for ckpt in range(2):
        flat_act = activations[ckpt].reshape(EXAMPLES * SEQ, FF)
        flat_grad = out_grads[ckpt].reshape(EXAMPLES * SEQ, D)
        low_in = jnp.dot(flat_act, proj_in, preferred_element_type=jnp.float32).astype(jnp.bfloat16)
        low_grad = jnp.dot(flat_grad, proj_out, preferred_element_type=jnp.float32).astype(jnp.bfloat16)
        low_in = low_in.reshape(EXAMPLES, SEQ, RANK).astype(jnp.float32)
        low_grad = low_grad.reshape(EXAMPLES, SEQ, RANK).astype(jnp.float32)
        outer = jnp.einsum('esa,esb->eab', low_in, low_grad) / jnp.sqrt(jnp.float32(SEQ))
        queries.append(outer.reshape(EXAMPLES, RANK * RANK).astype(jnp.bfloat16))
    scores = ckpt_rate[0] * jnp.dot(queries[0], store[0].T, preferred_element_type=jnp.float32)
    scores = scores + ckpt_rate[1] * jnp.dot(queries[1], store[1].T, preferred_element_type=jnp.float32)
    member = (store_group[:, None] == jnp.arange(GROUPS, dtype=jnp.int32)[None, :]).astype(jnp.float32)
    totals = jnp.dot(scores, member, precision=lax.Precision.HIGHEST)
    group_scores = totals / jnp.sqrt(jnp.float32(STORE) / jnp.float32(GROUPS))
    return (scores, group_scores)
```

```python
import functools
import jax
import jax.numpy as jnp
from jax import lax
from jax.experimental import pallas as pl
from jax.experimental.pallas import tpu as pltpu
from jax.sharding import PartitionSpec as P

GROUPS = 16
MESH = pl.DeviceIdType.MESH
NZ = 4
HALVES = 2
CUBE = ((1, 0, 0), (0, 1, 0), (1, 1, 0), (0, 0, 1), (1, 0, 1), (0, 1, 1), (1, 1, 1))
PLANE = ((1, 0), (0, 1), (1, 1))


def nt_dot(a, b, **kw):
    return lax.dot_general(
        a, b, (((1,), (1,)), ((), ())), preferred_element_type=jnp.float32, **kw
    )


def kernel(
    norm, scale,
    act, grad, pin, pout, store, rate, group,
    scores_o, group_o,
    abuf, gbuf, wi, wo, sbuf, part, sendb, recvb, piece, wide, q, tmp, t1, t2,
    load_sem, w_sem, store_sem, xs, xr, zs, zr, ps, pr, cs, cr, as_, ar, bs, br,
):
    dp = lax.axis_index("dp")
    x = lax.axis_index("mp")
    z = dp // 4
    y = (dp // 2) % 2
    c = dp % 2
    rank = pin.shape[0]
    ff = act.shape[3]
    cols = ff // HALVES

    def flip(v, on):
        return 1 - v if on else v

    def where_is(z_, y_, c_, x_):
        return ((z_ * 2 + y_) * 2 + c_, x_)

    def loads(p):
        ck = (1 - x) + (p // 2) * (2 * x - 1)
        e = p % 2
        out = [pltpu.make_async_copy(grad.at[ck, e], gbuf.at[p], load_sem.at[p, 0])]
        for h in range(HALVES):
            span = pl.ds(h * cols, cols)
            out.append(
                pltpu.make_async_copy(
                    act.at[ck, e, :, span], abuf.at[p, :, span], load_sem.at[p, 1 + h]
                )
            )
        return out

    w_in = pltpu.make_async_copy(pin, wi.at[pl.ds(0, rank)], w_sem.at[0])
    w_out = pltpu.make_async_copy(pout, wo.at[pl.ds(rank, rank)], w_sem.at[1])
    get_store = pltpu.make_async_copy(store, sbuf, store_sem)

    w_out.start()
    first = loads(0)
    first[0].start()
    w_in.start()
    for copy in first[1:]:
        copy.start()

    barrier = pltpu.get_barrier_semaphore()
    friends = [where_is((z + j) % NZ, y, c, x) for j in range(1, NZ)]
    friends += [where_is(z, flip(y, dy), flip(c, dc), flip(x, dx)) for dx, dy, dc in CUBE]
    for friend in friends:
        pl.semaphore_signal(barrier, inc=1, device_id=friend, device_id_type=MESH)

    wi[pl.ds(rank, rank), :] = jnp.zeros((rank, ff), wi.dtype)
    wo[pl.ds(0, rank), :] = jnp.zeros((rank, wo.shape[1]), wo.dtype)
    pl.semaphore_wait(barrier, len(friends))
    w_out.wait()
    w_in.wait()

    def partial_copy(p):
        return pltpu.make_async_remote_copy(
            sendb.at[p], recvb.at[p], xs.at[p], xr.at[p],
            device_id=where_is(z, y, c, 1 - x), device_id_type=MESH,
        )

    @pl.loop(0, 4)
    def _(p):
        @pl.when(p < 3)
        def _():
            for copy in loads(p + 1):
                copy.start()

        @pl.when(p == 3)
        def _():
            get_store.start()

        here = loads(p)
        here[0].wait()
        acc = nt_dot(gbuf[p], wo[...])
        for h in range(HALVES):
            here[1 + h].wait()
            acc += nt_dot(abuf[p, :, h * cols : (h + 1) * cols], wi[:, h * cols : (h + 1) * cols])

        @pl.when(p < 2)
        def _():
            sendb[p] = acc.astype(sendb.dtype)
            partial_copy(p).start()

        @pl.when(p >= 2)
        def _():
            part[p - 2] = acc

    def spot(z_, y_, c_, x_):
        return piece.at[x_, pl.ds(2 * ((z_ * 2 + y_) * 2 + c_), 2)]

    lane = lax.broadcasted_iota(jnp.int32, (rank // 2, 2 * rank), 1)
    for e in range(2):
        partial_copy(e).wait_recv()
        low = (part[e] + recvb[e].astype(jnp.float32)).astype(jnp.bfloat16)
        tmp[e] = lax.dot_general(
            low, low, (((0,), (0,)), ((), ())), preferred_element_type=jnp.float32
        )
        even = tmp[e, pl.ds(0, rank // 2, stride=2), :]
        odd = tmp[e, pl.ds(1, rank // 2, stride=2), :]
        flat = jnp.where(lane < rank, pltpu.roll(even, rank, 1), odd) * scale
        piece[x, 2 * dp + e] = flat.astype(piece.dtype)

    sent = []

    def send(owner, to, s_sem, r_sem):
        copy = pltpu.make_async_remote_copy(
            spot(*owner), spot(*owner), s_sem, r_sem, device_id=where_is(*to), device_id_type=MESH
        )
        copy.start()
        sent.append(copy)
        return copy

    rows = rank // 2

    def widen(owner):
        z_, y_, c_, x_ = owner
        first_row = pl.multiple_of(2 * ((z_ * 2 + y_) * 2 + c_) * rows, 2 * rows)
        wide[x_, pl.ds(first_row, 2 * rows), :] = (
            spot(*owner)[...].astype(jnp.float32).reshape(2 * rows, 2 * rank)
        )

    from_z, from_plane, from_core = {}, {}, []
    order = (0, 1, 3, 2)
    for j in (2, 1, 3):
        from_z[j] = send((z, y, c, x), ((z + j) % NZ, y, c, x), zs.at[j - 1], zr.at[j - 1])
    for k in order:
        zk = (z + NZ - k) % NZ
        if k:
            from_z[k].wait_recv()
        for d, (dx, dy) in enumerate(PLANE):
            from_plane[d, k] = send(
                (zk, y, c, x), (z, flip(y, dy), c, flip(x, dx)), ps.at[d, k], pr.at[d, k]
            )
        from_core.append(send((zk, y, c, x), (z, y, 1 - c, x), cs.at[3, k], cr.at[3, k]))
        widen((zk, y, c, x))
    for k in order:
        zk = (z + NZ - k) % NZ
        for d, (dx, dy) in enumerate(PLANE):
            from_plane[d, k].wait_recv()
            owner = (zk, flip(y, dy), c, flip(x, dx))
            from_core.append(send(owner, (z, y, 1 - c, x), cs.at[d, k], cr.at[d, k]))
            widen(owner)
    at = 0
    for k in order:
        from_core[at].wait_recv()
        at += 1
        widen(((z + NZ - k) % NZ, y, 1 - c, x))
    for k in order:
        for dx, dy in PLANE:
            from_core[at].wait_recv()
            at += 1
            widen(((z + NZ - k) % NZ, flip(y, dy), 1 - c, flip(x, dx)))

    examples = scores_o.shape[0]
    for ck in range(2):
        for kt in range(rows):
            q[ck, :, kt * 2 * rank : (kt + 1) * 2 * rank] = wide[
                ck, pl.ds(kt, examples, stride=rows), :
            ].astype(q.dtype)
    get_store.wait()
    scores = rate[0] * nt_dot(q[0], sbuf[0]) + rate[1] * nt_dot(q[1], sbuf[1])
    scores_o[...] = scores
    member = (
        lax.broadcasted_iota(jnp.int32, (GROUPS, scores.shape[1]), 0) == group[...]
    ).astype(jnp.float32)
    mine = z * 0 + (x * 2 + y) * 2 + c
    t1[mine, :, 0:examples] = nt_dot(member, scores, precision=lax.Precision.HIGHEST)
    round1 = []
    for j, (dx, dy, dc) in enumerate(CUBE):
        copy = pltpu.make_async_remote_copy(
            t1.at[mine], t1.at[mine], as_.at[j], ar.at[j],
            device_id=where_is(z, flip(y, dy), flip(c, dc), flip(x, dx)), device_id_type=MESH,
        )
        copy.start()
        round1.append(copy)
    for copy in round1:
        copy.wait_recv()
    total = t1[0]
    for j in range(1, 8):
        total += t1[j]
    t2[z] = total
    round2 = []
    for j in (2, 1, 3):
        copy = pltpu.make_async_remote_copy(
            t2.at[z], t2.at[z], bs.at[j - 1], br.at[j - 1],
            device_id=where_is((z + j) % NZ, y, c, x), device_id_type=MESH,
        )
        copy.start()
        round2.append(copy)
    for copy in round2:
        copy.wait_recv()
    total = t2[0]
    for j in range(1, NZ):
        total += t2[j]
    group_o[...] = total[:, 0:examples] * norm
    for p in range(2):
        partial_copy(p).wait_send()
    for copy in sent + round1 + round2:
        copy.wait_send()


def fused(activations, out_grads, proj_in, proj_out, store, ckpt_rate, store_group):
    ckpts, ex_local, seq_len, ff = activations.shape
    width = out_grads.shape[3]
    rank = proj_in.shape[1]
    devices = lax.axis_size("dp") * lax.axis_size("mp")
    examples = ex_local * lax.axis_size("dp")
    rows, depth = store.shape[1:]
    norm = (GROUPS / (rows * devices)) ** 0.5
    scale = seq_len ** -0.5
    hbm = pl.BlockSpec(memory_space=pltpu.HBM)
    vmem = pl.BlockSpec(memory_space=pltpu.VMEM)
    bf16, f32 = jnp.bfloat16, jnp.float32
    dma = pltpu.SemaphoreType.DMA
    scores, totals = pl.pallas_call(
        functools.partial(kernel, norm, scale),
        out_shape=(
            jax.ShapeDtypeStruct((examples, rows), f32),
            jax.ShapeDtypeStruct((GROUPS, examples), f32),
        ),
        in_specs=[hbm] * 5 + [pl.BlockSpec(memory_space=pltpu.SMEM), vmem],
        out_specs=(vmem, vmem),
        scratch_shapes=[
            pltpu.VMEM((4, seq_len, ff), bf16),
            pltpu.VMEM((4, seq_len, width), bf16),
            pltpu.VMEM((2 * rank, ff), bf16),
            pltpu.VMEM((2 * rank, width), bf16),
            pltpu.VMEM((ckpts, rows, depth), bf16),
            pltpu.VMEM((2, seq_len, 2 * rank), f32),
            pltpu.VMEM((2, seq_len, 2 * rank), bf16),
            pltpu.VMEM((2, seq_len, 2 * rank), bf16),
            pltpu.VMEM((ckpts, examples, rank // 2, 2 * rank), bf16),
            pltpu.VMEM((ckpts, examples * rank // 2, 2 * rank), f32),
            pltpu.VMEM((ckpts, examples, depth), bf16),
            pltpu.VMEM((2, 2 * rank, 2 * rank), f32),
            pltpu.VMEM((8, GROUPS, 128), f32),
            pltpu.VMEM((NZ, GROUPS, 128), f32),
            dma((4, 1 + HALVES)), dma((2,)), dma(()),
            dma((2,)), dma((2,)),
            dma((3,)), dma((3,)),
            dma((3, 4)), dma((3, 4)),
            dma((4, 4)), dma((4, 4)),
            dma((7,)), dma((7,)),
            dma((3,)), dma((3,)),
        ],
        compiler_params=pltpu.CompilerParams(
            collective_id=0, has_side_effects=True, vmem_limit_bytes=58 * 2**20
        ),
    )(
        activations, out_grads, proj_in.T, proj_out.T, store, ckpt_rate,
        store_group.reshape(1, rows),
    )
    return scores, totals.T


def shards(activations, out_grads, proj_in, proj_out, store, ckpt_rate, store_group):
    rank = proj_in.shape[1]
    seq_len = activations.shape[2]
    ex_local = activations.shape[1]
    scale = 1.0 / jnp.sqrt(jnp.float32(seq_len))
    part_in = jnp.einsum("cesf,fr->cesr", activations, proj_in, preferred_element_type=jnp.float32)
    part_out = jnp.einsum("cesf,fr->cesr", out_grads, proj_out, preferred_element_type=jnp.float32)
    stacked = jnp.concatenate([part_in, part_out], axis=3)
    summed = lax.psum(stacked, "mp")
    low_in = summed[..., :rank].astype(jnp.bfloat16)
    low_grad = summed[..., rank:].astype(jnp.bfloat16)
    outer = jnp.einsum("cesa,cesb->ecab", low_in, low_grad, preferred_element_type=jnp.float32)
    query = (outer.reshape(ex_local, 2, rank * rank) * scale).astype(jnp.bfloat16)
    gathered = lax.all_gather(query, "dp", axis=0, tiled=True)
    first = jnp.einsum("qk,rk->qr", gathered[:, 0], store[0], preferred_element_type=jnp.float32)
    second = jnp.einsum("qk,rk->qr", gathered[:, 1], store[1], preferred_element_type=jnp.float32)
    scores = ckpt_rate[0] * first + ckpt_rate[1] * second
    member = (store_group[:, None] == jnp.arange(GROUPS, dtype=jnp.int32)[None, :]).astype(
        jnp.float32
    )
    partial_totals = jnp.dot(scores, member, precision=lax.Precision.HIGHEST)
    totals = lax.psum(partial_totals, ("dp", "mp"))
    store_rows = store.shape[1] * lax.axis_size("dp") * lax.axis_size("mp")
    group_scores = totals / jnp.sqrt(jnp.float32(store_rows) / jnp.float32(GROUPS))
    return (scores, group_scores)


def solution(mesh):
    placed = (
        P(None, "dp", None, "mp"),
        P(None, "dp", None, "mp"),
        P("mp", None),
        P("mp", None),
        P(None, ("dp", "mp"), None),
        P(),
        P(("dp", "mp")),
    )
    small = mesh.shape["dp"] == 4 * NZ and mesh.shape["mp"] == 2
    return jax.shard_map(
        fused if small else shards,
        mesh=mesh, in_specs=placed, out_specs=(P(None, ("dp", "mp")), P()), check_vma=False,
    )
```

```python
import functools
import jax
import jax.numpy as jnp
from jax import lax
from jax.experimental import pallas as pl
from jax.experimental.pallas import tpu as pltpu
from jax.sharding import PartitionSpec as P

GROUPS = 16
MESH = pl.DeviceIdType.MESH
NZ = 4
CUTS = 4
CUBE = ((1, 0, 0), (0, 1, 0), (1, 1, 0), (0, 0, 1), (1, 0, 1), (0, 1, 1), (1, 1, 1))
PLANE = ((1, 0), (0, 1), (1, 1))


def nt_dot(a, b, **kw):
    return lax.dot_general(
        a, b, (((1,), (1,)), ((), ())), preferred_element_type=jnp.float32, **kw
    )


def kernel(
    norm, scale,
    act, grad, pin, pout, store, rate, group,
    scores_o, group_o,
    abuf, gbuf, wi, wo, sbuf, part, sendb, recvb, qsend, qrecv, piece, wide, q, tmp, t1, t2,
    load_sem, w_sem, store_sem, xs, xr, qs, qr, zs, zr, ps, pr, cs, cr, as_, ar, bs, br,
):
    dp = lax.axis_index("dp")
    x = lax.axis_index("mp")
    z = dp // 4
    y = (dp // 2) % 2
    c = dp % 2
    rank = pin.shape[0]
    ff = act.shape[3]
    cols = ff // CUTS

    def flip(v, on):
        return 1 - v if on else v

    def where_is(z_, y_, c_, x_):
        return ((z_ * 2 + y_) * 2 + c_, x_)

    def load(p, h):
        ck = (1 - x) + p * (2 * x - 1)
        if h == 0:
            return pltpu.make_async_copy(grad.at[ck], gbuf.at[p], load_sem.at[p, 0])
        span = pl.ds((h - 1) * cols, cols)
        return pltpu.make_async_copy(
            act.at[ck, :, :, span], abuf.at[p, :, :, span], load_sem.at[p, h]
        )

    w_in = pltpu.make_async_copy(pin, wi, w_sem.at[0])
    w_out = pltpu.make_async_copy(pout, wo, w_sem.at[1])
    get_store = pltpu.make_async_copy(store, sbuf, store_sem)

    w_out.start()
    load(0, 0).start()
    load(1, 0).start()
    w_in.start()
    for h in range(1, 1 + CUTS):
        load(0, h).start()

    barrier = pltpu.get_barrier_semaphore()
    friends = [where_is((z + j) % NZ, y, c, x) for j in range(1, NZ)]
    friends += [where_is(z, flip(y, dy), flip(c, dc), flip(x, dx)) for dx, dy, dc in CUBE]
    for friend in friends:
        pl.semaphore_signal(barrier, inc=1, device_id=friend, device_id_type=MESH)

    peer = where_is(z, y, c, 1 - x)
    seq = act.shape[2]

    def grad_copy(p):
        ck = (1 - x) + p * (2 * x - 1)
        return pltpu.make_async_remote_copy(
            sendb.at[ck], recvb.at[ck], xs.at[ck], xr.at[ck],
            device_id=peer, device_id_type=MESH,
        )

    query_copy = pltpu.make_async_remote_copy(
        qsend, qrecv, qs, qr, device_id=peer, device_id_type=MESH
    )

    w_out.wait()
    for p in range(2):
        ck = (1 - x) + p * (2 * x - 1)
        load(p, 0).wait()
        low = nt_dot(gbuf[p].reshape(2 * seq, gbuf.shape[3]), wo[...])
        low = jnp.concatenate([low[:seq], low[seq:]], axis=1)
        part[ck] = low
        sendb[ck] = low.astype(sendb.dtype)
        if p == 0:
            pl.semaphore_wait(barrier, len(friends))
        grad_copy(p).start()
    w_in.wait()
    side = lax.broadcasted_iota(jnp.int32, (rank, 2 * rank), 1)

    @pl.loop(0, 2)
    def _(p):
        acc = jnp.zeros((2 * seq, rank), jnp.float32)
        for h in range(1, 1 + CUTS):
            load(p, h).wait()

            @pl.when(p == 0)
            def _():
                load(1, h).start()

            span = slice((h - 1) * cols, h * cols)
            acc += nt_dot(abuf[p, :, :, span].reshape(2 * seq, cols), wi[:, span])
        acc = jnp.concatenate([acc[:seq], acc[seq:]], axis=1)

        @pl.when(p == 0)
        def _():
            get_store.start()
            for k in range(2):
                grad_copy(k).wait_recv()

        ck = (1 - x) + p * (2 * x - 1)
        low = part[ck] + recvb[ck].astype(jnp.float32)
        outer = lax.dot_general(
            acc, low, (((0,), (0,)), ((), ())),
            preferred_element_type=jnp.float32, precision=lax.Precision.HIGHEST,
        )
        outer = jnp.where(side < rank, outer[:rank], outer[rank:])

        @pl.when(p == 0)
        def _():
            qsend[...] = outer
            query_copy.start()

        @pl.when(p == 1)
        def _():
            tmp[...] = outer

    def spot(z_, y_, c_, x_):
        return piece.at[x_, pl.ds(2 * ((z_ * 2 + y_) * 2 + c_), 2)]

    lane = lax.broadcasted_iota(jnp.int32, (rank // 2, 2 * rank), 1)
    query_copy.wait_recv()
    tmp[...] += qrecv[...]
    even = tmp[pl.ds(0, rank // 2, stride=2), :]
    odd = tmp[pl.ds(1, rank // 2, stride=2), :]
    flat = (
        jnp.where(lane < rank, even, pltpu.roll(odd, rank, 1)),
        jnp.where(lane < rank, pltpu.roll(even, rank, 1), odd),
    )
    for e in range(2):
        piece[x, 2 * dp + e] = (flat[e] * scale).astype(piece.dtype)

    sent = []

    def send(owner, to, s_sem, r_sem):
        copy = pltpu.make_async_remote_copy(
            spot(*owner), spot(*owner), s_sem, r_sem, device_id=where_is(*to), device_id_type=MESH
        )
        copy.start()
        sent.append(copy)
        return copy

    rows = rank // 2

    def widen(owner):
        z_, y_, c_, x_ = owner
        first_row = pl.multiple_of(2 * ((z_ * 2 + y_) * 2 + c_) * rows, 2 * rows)
        wide[x_, pl.ds(first_row, 2 * rows), :] = (
            spot(*owner)[...].astype(jnp.float32).reshape(2 * rows, 2 * rank)
        )

    from_z, from_plane, from_core = {}, {}, []
    order = (0, 1, 3, 2)
    for j in (2, 1, 3):
        from_z[j] = send((z, y, c, x), ((z + j) % NZ, y, c, x), zs.at[j - 1], zr.at[j - 1])
    for k in order:
        zk = (z + NZ - k) % NZ
        if k:
            from_z[k].wait_recv()
        for d, (dx, dy) in enumerate(PLANE):
            from_plane[d, k] = send(
                (zk, y, c, x), (z, flip(y, dy), c, flip(x, dx)), ps.at[d, k], pr.at[d, k]
            )
        from_core.append(send((zk, y, c, x), (z, y, 1 - c, x), cs.at[3, k], cr.at[3, k]))
        widen((zk, y, c, x))
    for k in order:
        zk = (z + NZ - k) % NZ
        for d, (dx, dy) in enumerate(PLANE):
            from_plane[d, k].wait_recv()
            owner = (zk, flip(y, dy), c, flip(x, dx))
            from_core.append(send(owner, (z, y, 1 - c, x), cs.at[d, k], cr.at[d, k]))
            widen(owner)
    at = 0
    for k in order:
        from_core[at].wait_recv()
        at += 1
        widen(((z + NZ - k) % NZ, y, 1 - c, x))
    for k in order:
        for dx, dy in PLANE:
            from_core[at].wait_recv()
            at += 1
            widen(((z + NZ - k) % NZ, flip(y, dy), 1 - c, flip(x, dx)))

    examples = scores_o.shape[0]
    for ck in range(2):
        for kt in range(rows):
            q[ck, :, kt * 2 * rank : (kt + 1) * 2 * rank] = wide[
                ck, pl.ds(kt, examples, stride=rows), :
            ].astype(q.dtype)
    get_store.wait()
    scores = rate[0] * nt_dot(q[0], sbuf[0]) + rate[1] * nt_dot(q[1], sbuf[1])
    scores_o[...] = scores
    member = (
        lax.broadcasted_iota(jnp.int32, (GROUPS, scores.shape[1]), 0) == group[...]
    ).astype(jnp.float32)
    mine = z * 0 + (x * 2 + y) * 2 + c
    t1[mine, :, 0:examples] = nt_dot(member, scores, precision=lax.Precision.HIGHEST)
    round1 = []
    for j, (dx, dy, dc) in enumerate(CUBE):
        copy = pltpu.make_async_remote_copy(
            t1.at[mine], t1.at[mine], as_.at[j], ar.at[j],
            device_id=where_is(z, flip(y, dy), flip(c, dc), flip(x, dx)), device_id_type=MESH,
        )
        copy.start()
        round1.append(copy)
    for copy in round1:
        copy.wait_recv()
    total = t1[0]
    for j in range(1, 8):
        total += t1[j]
    t2[z] = total
    round2 = []
    for j in (2, 1, 3):
        copy = pltpu.make_async_remote_copy(
            t2.at[z], t2.at[z], bs.at[j - 1], br.at[j - 1],
            device_id=where_is((z + j) % NZ, y, c, x), device_id_type=MESH,
        )
        copy.start()
        round2.append(copy)
    for copy in round2:
        copy.wait_recv()
    total = t2[0]
    for j in range(1, NZ):
        total += t2[j]
    group_o[...] = total[:, 0:examples] * norm
    for p in range(2):
        grad_copy(p).wait_send()
    query_copy.wait_send()
    for copy in sent + round1 + round2:
        copy.wait_send()


def fused(activations, out_grads, proj_in, proj_out, store, ckpt_rate, store_group):
    ckpts, ex_local, seq_len, ff = activations.shape
    width = out_grads.shape[3]
    rank = proj_in.shape[1]
    devices = lax.axis_size("dp") * lax.axis_size("mp")
    examples = ex_local * lax.axis_size("dp")
    rows, depth = store.shape[1:]
    norm = (GROUPS / (rows * devices)) ** 0.5
    scale = seq_len ** -0.5
    hbm = pl.BlockSpec(memory_space=pltpu.HBM)
    vmem = pl.BlockSpec(memory_space=pltpu.VMEM)
    bf16, f32 = jnp.bfloat16, jnp.float32
    dma = pltpu.SemaphoreType.DMA
    scores, totals = pl.pallas_call(
        functools.partial(kernel, norm, scale),
        out_shape=(
            jax.ShapeDtypeStruct((examples, rows), f32),
            jax.ShapeDtypeStruct((GROUPS, examples), f32),
        ),
        in_specs=[hbm] * 5 + [pl.BlockSpec(memory_space=pltpu.SMEM), vmem],
        out_specs=(vmem, vmem),
        scratch_shapes=[
            pltpu.VMEM((2, 2, seq_len, ff), bf16),
            pltpu.VMEM((2, 2, seq_len, width), bf16),
            pltpu.VMEM((rank, ff), bf16),
            pltpu.VMEM((rank, width), bf16),
            pltpu.VMEM((ckpts, rows, depth), bf16),
            pltpu.VMEM((2, seq_len, 2 * rank), f32),
            pltpu.VMEM((2, seq_len, 2 * rank), bf16),
            pltpu.VMEM((2, seq_len, 2 * rank), bf16),
            pltpu.VMEM((rank, 2 * rank), f32),
            pltpu.VMEM((rank, 2 * rank), f32),
            pltpu.VMEM((ckpts, examples, rank // 2, 2 * rank), bf16),
            pltpu.VMEM((ckpts, examples * rank // 2, 2 * rank), f32),
            pltpu.VMEM((ckpts, examples, depth), bf16),
            pltpu.VMEM((rank, 2 * rank), f32),
            pltpu.VMEM((8, GROUPS, 128), f32),
            pltpu.VMEM((NZ, GROUPS, 128), f32),
            dma((2, 1 + CUTS)), dma((2,)), dma(()),
            dma((2,)), dma((2,)), dma(()), dma(()),
            dma((3,)), dma((3,)),
            dma((3, 4)), dma((3, 4)),
            dma((4, 4)), dma((4, 4)),
            dma((7,)), dma((7,)),
            dma((3,)), dma((3,)),
        ],
        compiler_params=pltpu.CompilerParams(
            collective_id=0, has_side_effects=True, vmem_limit_bytes=58 * 2**20
        ),
    )(
        activations, out_grads, proj_in.T, proj_out.T, store, ckpt_rate,
        store_group.reshape(1, rows),
    )
    return scores, totals.T


def shards(activations, out_grads, proj_in, proj_out, store, ckpt_rate, store_group):
    rank = proj_in.shape[1]
    seq_len = activations.shape[2]
    ex_local = activations.shape[1]
    scale = 1.0 / jnp.sqrt(jnp.float32(seq_len))
    part_in = jnp.einsum("cesf,fr->cesr", activations, proj_in, preferred_element_type=jnp.float32)
    part_out = jnp.einsum("cesf,fr->cesr", out_grads, proj_out, preferred_element_type=jnp.float32)
    stacked = jnp.concatenate([part_in, part_out], axis=3)
    summed = lax.psum(stacked, "mp")
    low_in = summed[..., :rank].astype(jnp.bfloat16)
    low_grad = summed[..., rank:].astype(jnp.bfloat16)
    outer = jnp.einsum("cesa,cesb->ecab", low_in, low_grad, preferred_element_type=jnp.float32)
    query = (outer.reshape(ex_local, 2, rank * rank) * scale).astype(jnp.bfloat16)
    gathered = lax.all_gather(query, "dp", axis=0, tiled=True)
    first = jnp.einsum("qk,rk->qr", gathered[:, 0], store[0], preferred_element_type=jnp.float32)
    second = jnp.einsum("qk,rk->qr", gathered[:, 1], store[1], preferred_element_type=jnp.float32)
    scores = ckpt_rate[0] * first + ckpt_rate[1] * second
    member = (store_group[:, None] == jnp.arange(GROUPS, dtype=jnp.int32)[None, :]).astype(
        jnp.float32
    )
    partial_totals = jnp.dot(scores, member, precision=lax.Precision.HIGHEST)
    totals = lax.psum(partial_totals, ("dp", "mp"))
    store_rows = store.shape[1] * lax.axis_size("dp") * lax.axis_size("mp")
    group_scores = totals / jnp.sqrt(jnp.float32(store_rows) / jnp.float32(GROUPS))
    return (scores, group_scores)


def solution(mesh):
    placed = (
        P(None, "dp", None, "mp"),
        P(None, "dp", None, "mp"),
        P("mp", None),
        P("mp", None),
        P(None, ("dp", "mp"), None),
        P(),
        P(("dp", "mp")),
    )
    small = mesh.shape["dp"] == 4 * NZ and mesh.shape["mp"] == 2
    return jax.shard_map(
        fused if small else shards,
        mesh=mesh, in_specs=placed, out_specs=(P(None, ("dp", "mp")), P()), check_vma=False,
    )
```

```python
import functools
import jax
import jax.numpy as jnp
from jax import lax
from jax.experimental import pallas as pl
from jax.experimental.pallas import tpu as pltpu
from jax.sharding import PartitionSpec as P

GROUPS = 16
MESH = pl.DeviceIdType.MESH
NZ = 4
DIRECT = (2,)
HALVES = 2
CUBE = ((1, 0, 0), (0, 1, 0), (1, 1, 0), (0, 0, 1), (1, 0, 1), (0, 1, 1), (1, 1, 1))
PLANE = ((1, 0), (0, 1), (1, 1))


def nt_dot(a, b, **kw):
    return lax.dot_general(
        a, b, (((1,), (1,)), ((), ())), preferred_element_type=jnp.float32, **kw
    )


def kernel(
    norm, scale,
    act, grad, pin, pout, store, rate, group,
    scores_o, group_o,
    abuf, gbuf, wi, wo, sbuf, part, sendb, recvb, piece, wide, q, tmp, t1, t2,
    load_sem, w_sem, store_sem, xs, xr, zs, zr, cs, cr, as_, ar, bs, br,
):
    dp = lax.axis_index("dp")
    x = lax.axis_index("mp")
    z = dp // 4
    y = (dp // 2) % 2
    c = dp % 2
    rank = pin.shape[0]
    ff = act.shape[3]
    cols = ff // HALVES

    def flip(v, on):
        return 1 - v if on else v

    def where_is(z_, y_, c_, x_):
        return ((z_ * 2 + y_) * 2 + c_, x_)

    def loads(p):
        ck = (1 - x) + (p // 2) * (2 * x - 1)
        e = p % 2
        out = [pltpu.make_async_copy(grad.at[ck, e], gbuf.at[p], load_sem.at[p, 0])]
        for h in range(HALVES):
            span = pl.ds(h * cols, cols)
            out.append(
                pltpu.make_async_copy(
                    act.at[ck, e, :, span], abuf.at[p, :, span], load_sem.at[p, 1 + h]
                )
            )
        return out

    w_in = pltpu.make_async_copy(pin, wi.at[pl.ds(0, rank)], w_sem.at[0])
    w_out = pltpu.make_async_copy(pout, wo.at[pl.ds(rank, rank)], w_sem.at[1])
    get_store = pltpu.make_async_copy(store, sbuf, store_sem)

    w_out.start()
    first = loads(0)
    first[0].start()
    w_in.start()
    for copy in first[1:]:
        copy.start()

    barrier = pltpu.get_barrier_semaphore()
    friends = [where_is((z + j) % NZ, y, c, x) for j in range(1, NZ)]
    friends += [where_is(z, flip(y, dy), flip(c, dc), flip(x, dx)) for dx, dy, dc in CUBE]
    for friend in friends:
        pl.semaphore_signal(barrier, inc=1, device_id=friend, device_id_type=MESH)

    wi[pl.ds(rank, rank), :] = jnp.zeros((rank, ff), wi.dtype)
    wo[pl.ds(0, rank), :] = jnp.zeros((rank, wo.shape[1]), wo.dtype)
    w_out.wait()
    w_in.wait()

    def partial_copy(p):
        return pltpu.make_async_remote_copy(
            sendb.at[p], recvb.at[p], xs.at[p], xr.at[p],
            device_id=where_is(z, y, c, 1 - x), device_id_type=MESH,
        )

    @pl.loop(0, 4)
    def _(p):
        @pl.when(p < 3)
        def _():
            for copy in loads(p + 1):
                copy.start()

        @pl.when(p == 3)
        def _():
            get_store.start()

        here = loads(p)
        here[0].wait()
        acc = nt_dot(gbuf[p], wo[...])
        for h in range(HALVES):
            here[1 + h].wait()
            acc += nt_dot(abuf[p, :, h * cols : (h + 1) * cols], wi[:, h * cols : (h + 1) * cols])

        @pl.when(p < 2)
        def _():
            sendb[p] = acc.astype(sendb.dtype)

            @pl.when(p == 0)
            def _():
                pl.semaphore_wait(barrier, len(friends))

            partial_copy(p).start()

        @pl.when(p >= 2)
        def _():
            part[p - 2] = acc

    def spot(z_, y_, c_, x_):
        return piece.at[x_, pl.ds(2 * ((z_ * 2 + y_) * 2 + c_), 2)]

    lane = lax.broadcasted_iota(jnp.int32, (rank // 2, 2 * rank), 1)
    for e in range(2):
        partial_copy(e).wait_recv()
        low = (part[e] + recvb[e].astype(jnp.float32)).astype(jnp.bfloat16)
        tmp[e] = lax.dot_general(
            low, low, (((0,), (0,)), ((), ())), preferred_element_type=jnp.float32
        )
        even = tmp[e, pl.ds(0, rank // 2, stride=2), :]
        odd = tmp[e, pl.ds(1, rank // 2, stride=2), :]
        flat = jnp.where(lane < rank, pltpu.roll(even, rank, 1), odd) * scale
        piece[x, 2 * dp + e] = flat.astype(piece.dtype)

    sent = []

    def send(owner, to, s_sem, r_sem):
        copy = pltpu.make_async_remote_copy(
            spot(*owner), spot(*owner), s_sem, r_sem, device_id=where_is(*to), device_id_type=MESH
        )
        copy.start()
        sent.append(copy)
        return copy

    rows = rank // 2

    def widen(owner):
        z_, y_, c_, x_ = owner
        first_row = pl.multiple_of(2 * ((z_ * 2 + y_) * 2 + c_) * rows, 2 * rows)
        wide[x_, pl.ds(first_row, 2 * rows), :] = (
            spot(*owner)[...].astype(jnp.float32).reshape(2 * rows, 2 * rank)
        )

    from_z, arriving, onward = {}, [], []
    order = (0, 1, 3, 2)
    for j in (2, 1, 3):
        from_z[j] = send((z, y, c, x), ((z + j) % NZ, y, c, x), zs.at[j - 1], zr.at[j - 1])
    for k in order:
        zk = (z + NZ - k) % NZ
        if k:
            from_z[k].wait_recv()
        for j, (dx, dy, dc) in enumerate(CUBE):
            if dc and (dx or dy) and k not in DIRECT:
                continue
            to = (z, flip(y, dy), flip(c, dc), flip(x, dx))
            copy = send((zk, y, c, x), to, cs.at[j, k], cr.at[j, k])
            source = (zk, flip(y, dy), flip(c, dc), flip(x, dx))
            if not dc and k not in DIRECT:
                onward.append((copy, source, j + 4, k))
            else:
                arriving.append((copy, source))
        widen((zk, y, c, x))
    for copy, source, j, k in onward:
        copy.wait_recv()
        again = send(source, (z, y, 1 - c, x), cs.at[j, k], cr.at[j, k])
        arriving.append((again, (source[0], source[1], 1 - c, source[3])))
        widen(source)
    for copy, source in arriving:
        copy.wait_recv()
        widen(source)

    examples = scores_o.shape[0]
    for ck in range(2):
        for kt in range(rows):
            q[ck, :, kt * 2 * rank : (kt + 1) * 2 * rank] = wide[
                ck, pl.ds(kt, examples, stride=rows), :
            ].astype(q.dtype)
    get_store.wait()
    scores = rate[0] * nt_dot(q[0], sbuf[0]) + rate[1] * nt_dot(q[1], sbuf[1])
    scores_o[...] = scores
    member = (
        lax.broadcasted_iota(jnp.int32, (GROUPS, scores.shape[1]), 0) == group[...]
    ).astype(jnp.float32)
    mine = z * 0 + (x * 2 + y) * 2 + c
    half = GROUPS // 2
    own = nt_dot(member, scores, precision=lax.Precision.HIGHEST)
    t1[mine, :, 0:examples] = own[:half]
    t1[mine, :, examples : 2 * examples] = own[half:]
    round1 = []
    for j, (dx, dy, dc) in enumerate(CUBE):
        copy = pltpu.make_async_remote_copy(
            t1.at[mine], t1.at[mine], as_.at[j], ar.at[j],
            device_id=where_is(z, flip(y, dy), flip(c, dc), flip(x, dx)), device_id_type=MESH,
        )
        copy.start()
        round1.append(copy)
    for copy in round1:
        copy.wait_recv()
    total = t1[0]
    for j in range(1, 8):
        total += t1[j]
    t2[z] = total
    round2 = []
    for j in (2, 1, 3):
        copy = pltpu.make_async_remote_copy(
            t2.at[z], t2.at[z], bs.at[j - 1], br.at[j - 1],
            device_id=where_is((z + j) % NZ, y, c, x), device_id_type=MESH,
        )
        copy.start()
        round2.append(copy)
    for copy in round2:
        copy.wait_recv()
    total = t2[0]
    for j in range(1, NZ):
        total += t2[j]
    group_o[:half, :] = total[:, 0:examples] * norm
    group_o[half:, :] = total[:, examples : 2 * examples] * norm
    for p in range(2):
        partial_copy(p).wait_send()
    for copy in sent + round1 + round2:
        copy.wait_send()


def fused(activations, out_grads, proj_in, proj_out, store, ckpt_rate, store_group):
    ckpts, ex_local, seq_len, ff = activations.shape
    width = out_grads.shape[3]
    rank = proj_in.shape[1]
    devices = lax.axis_size("dp") * lax.axis_size("mp")
    examples = ex_local * lax.axis_size("dp")
    rows, depth = store.shape[1:]
    norm = (GROUPS / (rows * devices)) ** 0.5
    scale = seq_len ** -0.5
    hbm = pl.BlockSpec(memory_space=pltpu.HBM)
    vmem = pl.BlockSpec(memory_space=pltpu.VMEM)
    bf16, f32 = jnp.bfloat16, jnp.float32
    dma = pltpu.SemaphoreType.DMA
    scores, totals = pl.pallas_call(
        functools.partial(kernel, norm, scale),
        out_shape=(
            jax.ShapeDtypeStruct((examples, rows), f32),
            jax.ShapeDtypeStruct((GROUPS, examples), f32),
        ),
        in_specs=[hbm] * 5 + [pl.BlockSpec(memory_space=pltpu.SMEM), vmem],
        out_specs=(vmem, vmem),
        scratch_shapes=[
            pltpu.VMEM((4, seq_len, ff), bf16),
            pltpu.VMEM((4, seq_len, width), bf16),
            pltpu.VMEM((2 * rank, ff), bf16),
            pltpu.VMEM((2 * rank, width), bf16),
            pltpu.VMEM((ckpts, rows, depth), bf16),
            pltpu.VMEM((2, seq_len, 2 * rank), f32),
            pltpu.VMEM((2, seq_len, 2 * rank), bf16),
            pltpu.VMEM((2, seq_len, 2 * rank), bf16),
            pltpu.VMEM((ckpts, examples, rank // 2, 2 * rank), bf16),
            pltpu.VMEM((ckpts, examples * rank // 2, 2 * rank), f32),
            pltpu.VMEM((ckpts, examples, depth), bf16),
            pltpu.VMEM((2, 2 * rank, 2 * rank), f32),
            pltpu.VMEM((8, GROUPS // 2, 128), f32),
            pltpu.VMEM((NZ, GROUPS // 2, 128), f32),
            dma((4, 1 + HALVES)), dma((2,)), dma(()),
            dma((2,)), dma((2,)),
            dma((3,)), dma((3,)),
                        dma((7, 4)), dma((7, 4)),
            dma((7,)), dma((7,)),
            dma((3,)), dma((3,)),
        ],
        compiler_params=pltpu.CompilerParams(
            collective_id=0, has_side_effects=True, vmem_limit_bytes=58 * 2**20
        ),
    )(
        activations, out_grads, proj_in.T, proj_out.T, store, ckpt_rate,
        store_group.reshape(1, rows),
    )
    return scores, totals.T


def shards(activations, out_grads, proj_in, proj_out, store, ckpt_rate, store_group):
    rank = proj_in.shape[1]
    seq_len = activations.shape[2]
    ex_local = activations.shape[1]
    scale = 1.0 / jnp.sqrt(jnp.float32(seq_len))
    part_in = jnp.einsum("cesf,fr->cesr", activations, proj_in, preferred_element_type=jnp.float32)
    part_out = jnp.einsum("cesf,fr->cesr", out_grads, proj_out, preferred_element_type=jnp.float32)
    stacked = jnp.concatenate([part_in, part_out], axis=3)
    summed = lax.psum(stacked, "mp")
    low_in = summed[..., :rank].astype(jnp.bfloat16)
    low_grad = summed[..., rank:].astype(jnp.bfloat16)
    outer = jnp.einsum("cesa,cesb->ecab", low_in, low_grad, preferred_element_type=jnp.float32)
    query = (outer.reshape(ex_local, 2, rank * rank) * scale).astype(jnp.bfloat16)
    gathered = lax.all_gather(query, "dp", axis=0, tiled=True)
    first = jnp.einsum("qk,rk->qr", gathered[:, 0], store[0], preferred_element_type=jnp.float32)
    second = jnp.einsum("qk,rk->qr", gathered[:, 1], store[1], preferred_element_type=jnp.float32)
    scores = ckpt_rate[0] * first + ckpt_rate[1] * second
    member = (store_group[:, None] == jnp.arange(GROUPS, dtype=jnp.int32)[None, :]).astype(
        jnp.float32
    )
    partial_totals = jnp.dot(scores, member, precision=lax.Precision.HIGHEST)
    totals = lax.psum(partial_totals, ("dp", "mp"))
    store_rows = store.shape[1] * lax.axis_size("dp") * lax.axis_size("mp")
    group_scores = totals / jnp.sqrt(jnp.float32(store_rows) / jnp.float32(GROUPS))
    return (scores, group_scores)


def solution(mesh):
    placed = (
        P(None, "dp", None, "mp"),
        P(None, "dp", None, "mp"),
        P("mp", None),
        P("mp", None),
        P(None, ("dp", "mp"), None),
        P(),
        P(("dp", "mp")),
    )
    small = mesh.shape["dp"] == 4 * NZ and mesh.shape["mp"] == 2
    return jax.shard_map(
        fused if small else shards,
        mesh=mesh, in_specs=placed, out_specs=(P(None, ("dp", "mp")), P()), check_vma=False,
    )
```

```python
import functools
import jax
import jax.numpy as jnp
from jax import lax
from jax.experimental import pallas as pl
from jax.experimental.pallas import tpu as pltpu
from jax.sharding import PartitionSpec as P

GROUPS = 16
MESH = pl.DeviceIdType.MESH
NZ = 4
DIRECT = (3, 2)
HALVES = 2
CUBE = ((1, 0, 0), (0, 1, 0), (1, 1, 0), (0, 0, 1), (1, 0, 1), (0, 1, 1), (1, 1, 1))
PLANE = ((1, 0), (0, 1), (1, 1))


def nt_dot(a, b, **kw):
    return lax.dot_general(
        a, b, (((1,), (1,)), ((), ())), preferred_element_type=jnp.float32, **kw
    )


def kernel(
    norm, scale,
    act, grad, pin, pout, store, rate, group,
    scores_o, group_o,
    abuf, gbuf, wi, wo, sbuf, part, sendb, recvb, piece, wide, q, tmp, t1, t2,
    load_sem, w_sem, store_sem, xs, xr, zs, zr, cs, cr, as_, ar, bs, br,
):
    dp = lax.axis_index("dp")
    x = lax.axis_index("mp")
    z = dp // 4
    y = (dp // 2) % 2
    c = dp % 2
    rank = pin.shape[0]
    ff = act.shape[3]
    cols = ff // HALVES

    def flip(v, on):
        return 1 - v if on else v

    def where_is(z_, y_, c_, x_):
        return ((z_ * 2 + y_) * 2 + c_, x_)

    def loads(p):
        ck = (1 - x) + (p // 2) * (2 * x - 1)
        e = p % 2
        out = [pltpu.make_async_copy(grad.at[ck, e], gbuf.at[p], load_sem.at[p, 0])]
        for h in range(HALVES):
            span = pl.ds(h * cols, cols)
            out.append(
                pltpu.make_async_copy(
                    act.at[ck, e, :, span], abuf.at[p, :, span], load_sem.at[p, 1 + h]
                )
            )
        return out

    w_in = pltpu.make_async_copy(pin, wi.at[pl.ds(0, rank)], w_sem.at[0])
    w_out = pltpu.make_async_copy(pout, wo.at[pl.ds(rank, rank)], w_sem.at[1])
    get_store = pltpu.make_async_copy(store, sbuf, store_sem)

    w_out.start()
    first = loads(0)
    first[0].start()
    w_in.start()
    for copy in first[1:]:
        copy.start()

    barrier = pltpu.get_barrier_semaphore()
    friends = [where_is((z + j) % NZ, y, c, x) for j in range(1, NZ)]
    friends += [where_is(z, flip(y, dy), flip(c, dc), flip(x, dx)) for dx, dy, dc in CUBE]
    for friend in friends:
        pl.semaphore_signal(barrier, inc=1, device_id=friend, device_id_type=MESH)

    wi[pl.ds(rank, rank), :] = jnp.zeros((rank, ff), wi.dtype)
    wo[pl.ds(0, rank), :] = jnp.zeros((rank, wo.shape[1]), wo.dtype)
    w_out.wait()
    w_in.wait()

    def partial_copy(p):
        return pltpu.make_async_remote_copy(
            sendb.at[p], recvb.at[p], xs.at[p], xr.at[p],
            device_id=where_is(z, y, c, 1 - x), device_id_type=MESH,
        )

    @pl.loop(0, 4)
    def _(p):
        @pl.when(p < 3)
        def _():
            for copy in loads(p + 1):
                copy.start()

        @pl.when(p == 3)
        def _():
            get_store.start()

        here = loads(p)
        here[0].wait()
        acc = nt_dot(gbuf[p], wo[...])
        for h in range(HALVES):
            here[1 + h].wait()
            acc += nt_dot(abuf[p, :, h * cols : (h + 1) * cols], wi[:, h * cols : (h + 1) * cols])

        @pl.when(p < 2)
        def _():
            sendb[p] = acc.astype(sendb.dtype)

            @pl.when(p == 0)
            def _():
                pl.semaphore_wait(barrier, len(friends))

            partial_copy(p).start()

        @pl.when(p >= 2)
        def _():
            part[p - 2] = acc

    def spot(z_, y_, c_, x_):
        return piece.at[x_, pl.ds(2 * ((z_ * 2 + y_) * 2 + c_), 2)]

    lane = lax.broadcasted_iota(jnp.int32, (rank // 2, 2 * rank), 1)
    for e in range(2):
        partial_copy(e).wait_recv()
        low = (part[e] + recvb[e].astype(jnp.float32)).astype(jnp.bfloat16)
        tmp[e] = lax.dot_general(
            low, low, (((0,), (0,)), ((), ())), preferred_element_type=jnp.float32
        )
        even = tmp[e, pl.ds(0, rank // 2, stride=2), :]
        odd = tmp[e, pl.ds(1, rank // 2, stride=2), :]
        flat = jnp.where(lane < rank, pltpu.roll(even, rank, 1), odd) * scale
        piece[x, 2 * dp + e] = flat.astype(piece.dtype)

    sent = []

    def send(owner, to, s_sem, r_sem):
        copy = pltpu.make_async_remote_copy(
            spot(*owner), spot(*owner), s_sem, r_sem, device_id=where_is(*to), device_id_type=MESH
        )
        copy.start()
        sent.append(copy)
        return copy

    rows = rank // 2

    def widen(owner):
        z_, y_, c_, x_ = owner
        first_row = pl.multiple_of(2 * ((z_ * 2 + y_) * 2 + c_) * rows, 2 * rows)
        wide[x_, pl.ds(first_row, 2 * rows), :] = (
            spot(*owner)[...].astype(jnp.float32).reshape(2 * rows, 2 * rank)
        )

    from_z, arriving, onward = {}, [], []
    order = (0, 1, 3, 2)
    for j in (2, 1, 3):
        from_z[j] = send((z, y, c, x), ((z + j) % NZ, y, c, x), zs.at[j - 1], zr.at[j - 1])
    for k in order:
        zk = (z + NZ - k) % NZ
        if k:
            from_z[k].wait_recv()
        for j, (dx, dy, dc) in enumerate(CUBE):
            if dc and (dx or dy) and k not in DIRECT:
                continue
            to = (z, flip(y, dy), flip(c, dc), flip(x, dx))
            copy = send((zk, y, c, x), to, cs.at[j, k], cr.at[j, k])
            source = (zk, flip(y, dy), flip(c, dc), flip(x, dx))
            if not dc and k not in DIRECT:
                onward.append((copy, source, j + 4, k))
            else:
                arriving.append((copy, source))
        widen((zk, y, c, x))
    for copy, source, j, k in onward:
        copy.wait_recv()
        again = send(source, (z, y, 1 - c, x), cs.at[j, k], cr.at[j, k])
        arriving.append((again, (source[0], source[1], 1 - c, source[3])))
        widen(source)
    for copy, source in arriving:
        copy.wait_recv()
        widen(source)

    examples = scores_o.shape[0]
    for ck in range(2):
        for kt in range(rows):
            q[ck, :, kt * 2 * rank : (kt + 1) * 2 * rank] = wide[
                ck, pl.ds(kt, examples, stride=rows), :
            ].astype(q.dtype)
    get_store.wait()
    scores = rate[0] * nt_dot(q[0], sbuf[0]) + rate[1] * nt_dot(q[1], sbuf[1])
    scores_o[...] = scores
    member = (
        lax.broadcasted_iota(jnp.int32, (GROUPS, scores.shape[1]), 0) == group[...]
    ).astype(jnp.float32)
    mine = z * 0 + (x * 2 + y) * 2 + c
    half = GROUPS // 2
    own = nt_dot(member, scores, precision=lax.Precision.HIGHEST)
    t1[mine, :, 0:examples] = own[:half]
    t1[mine, :, examples : 2 * examples] = own[half:]
    round1 = []
    for j, (dx, dy, dc) in enumerate(CUBE):
        copy = pltpu.make_async_remote_copy(
            t1.at[mine], t1.at[mine], as_.at[j], ar.at[j],
            device_id=where_is(z, flip(y, dy), flip(c, dc), flip(x, dx)), device_id_type=MESH,
        )
        copy.start()
        round1.append(copy)
    for copy in round1:
        copy.wait_recv()
    total = t1[0]
    for j in range(1, 8):
        total += t1[j]
    t2[z] = total
    round2 = []
    for j in (2, 1, 3):
        copy = pltpu.make_async_remote_copy(
            t2.at[z], t2.at[z], bs.at[j - 1], br.at[j - 1],
            device_id=where_is((z + j) % NZ, y, c, x), device_id_type=MESH,
        )
        copy.start()
        round2.append(copy)
    for copy in round2:
        copy.wait_recv()
    total = t2[0]
    for j in range(1, NZ):
        total += t2[j]
    group_o[:half, :] = total[:, 0:examples] * norm
    group_o[half:, :] = total[:, examples : 2 * examples] * norm
    for p in range(2):
        partial_copy(p).wait_send()
    for copy in sent + round1 + round2:
        copy.wait_send()


def fused(activations, out_grads, proj_in, proj_out, store, ckpt_rate, store_group):
    ckpts, ex_local, seq_len, ff = activations.shape
    width = out_grads.shape[3]
    rank = proj_in.shape[1]
    devices = lax.axis_size("dp") * lax.axis_size("mp")
    examples = ex_local * lax.axis_size("dp")
    rows, depth = store.shape[1:]
    norm = (GROUPS / (rows * devices)) ** 0.5
    scale = seq_len ** -0.5
    hbm = pl.BlockSpec(memory_space=pltpu.HBM)
    vmem = pl.BlockSpec(memory_space=pltpu.VMEM)
    bf16, f32 = jnp.bfloat16, jnp.float32
    dma = pltpu.SemaphoreType.DMA
    scores, totals = pl.pallas_call(
        functools.partial(kernel, norm, scale),
        out_shape=(
            jax.ShapeDtypeStruct((examples, rows), f32),
            jax.ShapeDtypeStruct((GROUPS, examples), f32),
        ),
        in_specs=[hbm] * 5 + [pl.BlockSpec(memory_space=pltpu.SMEM), vmem],
        out_specs=(vmem, vmem),
        scratch_shapes=[
            pltpu.VMEM((4, seq_len, ff), bf16),
            pltpu.VMEM((4, seq_len, width), bf16),
            pltpu.VMEM((2 * rank, ff), bf16),
            pltpu.VMEM((2 * rank, width), bf16),
            pltpu.VMEM((ckpts, rows, depth), bf16),
            pltpu.VMEM((2, seq_len, 2 * rank), f32),
            pltpu.VMEM((2, seq_len, 2 * rank), bf16),
            pltpu.VMEM((2, seq_len, 2 * rank), bf16),
            pltpu.VMEM((ckpts, examples, rank // 2, 2 * rank), bf16),
            pltpu.VMEM((ckpts, examples * rank // 2, 2 * rank), f32),
            pltpu.VMEM((ckpts, examples, depth), bf16),
            pltpu.VMEM((2, 2 * rank, 2 * rank), f32),
            pltpu.VMEM((8, GROUPS // 2, 128), f32),
            pltpu.VMEM((NZ, GROUPS // 2, 128), f32),
            dma((4, 1 + HALVES)), dma((2,)), dma(()),
            dma((2,)), dma((2,)),
            dma((3,)), dma((3,)),
                        dma((7, 4)), dma((7, 4)),
            dma((7,)), dma((7,)),
            dma((3,)), dma((3,)),
        ],
        compiler_params=pltpu.CompilerParams(
            collective_id=0, has_side_effects=True, vmem_limit_bytes=58 * 2**20
        ),
    )(
        activations, out_grads, proj_in.T, proj_out.T, store, ckpt_rate,
        store_group.reshape(1, rows),
    )
    return scores, totals.T


def shards(activations, out_grads, proj_in, proj_out, store, ckpt_rate, store_group):
    rank = proj_in.shape[1]
    seq_len = activations.shape[2]
    ex_local = activations.shape[1]
    scale = 1.0 / jnp.sqrt(jnp.float32(seq_len))
    part_in = jnp.einsum("cesf,fr->cesr", activations, proj_in, preferred_element_type=jnp.float32)
    part_out = jnp.einsum("cesf,fr->cesr", out_grads, proj_out, preferred_element_type=jnp.float32)
    stacked = jnp.concatenate([part_in, part_out], axis=3)
    summed = lax.psum(stacked, "mp")
    low_in = summed[..., :rank].astype(jnp.bfloat16)
    low_grad = summed[..., rank:].astype(jnp.bfloat16)
    outer = jnp.einsum("cesa,cesb->ecab", low_in, low_grad, preferred_element_type=jnp.float32)
    query = (outer.reshape(ex_local, 2, rank * rank) * scale).astype(jnp.bfloat16)
    gathered = lax.all_gather(query, "dp", axis=0, tiled=True)
    first = jnp.einsum("qk,rk->qr", gathered[:, 0], store[0], preferred_element_type=jnp.float32)
    second = jnp.einsum("qk,rk->qr", gathered[:, 1], store[1], preferred_element_type=jnp.float32)
    scores = ckpt_rate[0] * first + ckpt_rate[1] * second
    member = (store_group[:, None] == jnp.arange(GROUPS, dtype=jnp.int32)[None, :]).astype(
        jnp.float32
    )
    partial_totals = jnp.dot(scores, member, precision=lax.Precision.HIGHEST)
    totals = lax.psum(partial_totals, ("dp", "mp"))
    store_rows = store.shape[1] * lax.axis_size("dp") * lax.axis_size("mp")
    group_scores = totals / jnp.sqrt(jnp.float32(store_rows) / jnp.float32(GROUPS))
    return (scores, group_scores)


def solution(mesh):
    placed = (
        P(None, "dp", None, "mp"),
        P(None, "dp", None, "mp"),
        P("mp", None),
        P("mp", None),
        P(None, ("dp", "mp"), None),
        P(),
        P(("dp", "mp")),
    )
    small = mesh.shape["dp"] == 4 * NZ and mesh.shape["mp"] == 2
    return jax.shard_map(
        fused if small else shards,
        mesh=mesh, in_specs=placed, out_specs=(P(None, ("dp", "mp")), P()), check_vma=False,
    )
```
